32 devices in a mesh: proto: 16 (over z, x, core), sample: 2 (over y).
Axes of the slice: x: 2, y: 2, z: 4, core: 2. Of those that a mesh axis runs over, the one named last changes fastest.
Arguments:
- teacher_new: bfloat16 [512, 384], P('sample'), may hold values from -6 to 6
- queue: bfloat16 [1536, 384], P('sample'), may hold values from -6 to 6
- student: bfloat16 [512, 384], P('sample'), may hold values from -6 to 6
- prototypes: bfloat16 [32768, 384], P('proto'), may hold values from -1 to 1
- owners: int32 [512, 1], P('sample'), may hold values from 0 to 1; in each aligned block of 256 rows (0 to 255, 256 to 511, ...) at most 256 rows name the same one
- queue_oldest_slot: int32 [2], P('sample'), may hold values from 0 to 767
Outputs:
- new_queue: bfloat16 [1536, 384], P('sample')
- proto_grad: float32 [32768, 384], P(('proto', 'sample'))
- loss: float32 [], replicated
The draws below stay inside these ranges and needn't reach their ends.
Inputs may be any that keep to these rules, and one draw needn't show every extreme that they name: `owners`: among the rows of one device (aligned blocks of 256 rows), no owner is named more than 256 times, a bound that some block reaches.
All inputs are finite; a program needn't handle non-finite values.
Results may differ from the reference program's by a relative error of at most 0.0034.
Values may be sent and summed in bfloat16 or wider, within the bound.
A program may use at most 64 MiB of HBM per device.

```python
import math
import jax
import jax.numpy as jnp
import numpy as np
from jax import lax

FEATURE_WIDTH = 384
K_DEV = 2048
NEW_DEV = 256
ITERS = 3
QUEUE_PER_INDEX = 768
CAP = 256
PROTOTYPE_COUNT = 32768
NEW_ROWS = 512
QUEUE = 1536
TEACHERS = 2048
GRAD_SCALE = 262144
N_PROTO = 16
N_SAMPLE = 2


group_count = 8


def cluster_centers(key):
    return jax.random.normal(jax.random.fold_in(key, 101), (group_count, FEATURE_WIDTH), jnp.float32)


def cluster_labels(key, salt, rows):
    first = jax.random.randint(jax.random.fold_in(key, salt), (rows,), 0, group_count)
    second = jax.random.randint(jax.random.fold_in(key, salt + 1), (rows,), 0, group_count)
    return jnp.minimum(first, second)


def mixed_rows(key, labels, salt, strength, rows):
    centers = jnp.take(cluster_centers(key), labels, axis=0)
    noise_key = jax.random.fold_in(key, salt)
    noise = jax.random.normal(noise_key, (rows, FEATURE_WIDTH), jnp.float32)
    return strength * centers + jnp.sqrt(1.0 - strength * strength) * noise


def teacher_rows(key, salt, rows):
    labels = cluster_labels(key, salt, rows)
    strength = 0.6
    return jnp.clip(mixed_rows(key, labels, salt + 7, strength, rows), -6.0, 6.0)


def draw_teacher_new(key, part):
    return teacher_rows(key, 202, NEW_ROWS).astype(jnp.bfloat16)


def draw_queue(key, part):
    return teacher_rows(key, 303, QUEUE).astype(jnp.bfloat16)


def draw_student(key, part):
    labels = cluster_labels(key, 202, NEW_ROWS)
    strength = 0.3
    values = mixed_rows(key, labels, 404, strength, NEW_ROWS)
    return jnp.clip(values, -6.0, 6.0).astype(jnp.bfloat16)


def draw_prototypes(key, part):
    labels = jax.random.randint(jax.random.fold_in(key, 505), (PROTOTYPE_COUNT,), 0, group_count)
    position = jnp.arange(PROTOTYPE_COUNT, dtype=jnp.float32)[:, None] / (PROTOTYPE_COUNT - 1.0)
    strength = 0.1 + 0.7 * position * position
    values = mixed_rows(key, labels, 707, strength, PROTOTYPE_COUNT) / math.sqrt(FEATURE_WIDTH)
    return jnp.clip(values, -1.0, 1.0).astype(jnp.bfloat16)


def assign_block(stream_key, own, number, rows, amount, top, limit, skew):
    ranking = jax.random.permutation(stream_key, amount)
    heavy_load, usual = load_shares(amount, rows * top, limit, skew, True), load_shares(amount, rows * top, limit, skew, False)
    places = jnp.arange(amount)

    def named(lengths, rotation):
        used = int((lengths > 0).sum())
        fixed = max(1, used // 4)
        shifted = fixed + (places - fixed + rotation * (used - fixed)) % max(1, amount - fixed)
        return jnp.zeros((amount,), jnp.int32).at[ranking[jnp.where(places < fixed, places, shifted)]].set(jnp.asarray(lengths, jnp.int32))

    lengths = jnp.where(number % 4 == 0, named(heavy_load, number // 4), named(usual, number - number // 4 - 1))
    mixed = jax.random.permutation(jax.random.fold_in(own, 3), amount)
    donor, receiver = mixed[0:amount // 2 * 2:2], mixed[1:amount // 2 * 2:2]
    room = jnp.minimum(lengths[donor] - 1, limit - lengths[receiver]) // 2
    room = jnp.where((donor == ranking[0]) | (receiver == ranking[0]) | (lengths[receiver] == 0), 0, jnp.maximum(room, 0))
    shifted = jax.random.randint(jax.random.fold_in(own, 4), (amount // 2,), 0, 1 << 20) % (room + 1)
    lengths = lengths.at[donor].add(-shifted).at[receiver].add(shifted)
    items = jnp.searchsorted(jnp.cumsum(lengths), jnp.arange(rows * top), side="right").astype(jnp.int32)
    listing = items.reshape(top, rows).T
    listing = listing[jax.random.permutation(jax.random.fold_in(own, 1), rows)]
    rotation = jax.random.randint(jax.random.fold_in(own, 2), (rows, 1), 0, top)
    return jnp.take_along_axis(listing, (jnp.arange(top)[None, :] + rotation) % top, axis=1)


def load_shares(count, total, bound, slope, full):
    loads = [(1 << 20) // math.isqrt(rank ** slope) + 1 for rank in range(1, count + 1)]
    largest = bound if full else min(bound, max(-(-total // count), total * loads[0] // sum(loads)))
    least = 1 if total - largest >= count - 1 else 0
    counts, rest = [largest] + [least] * (count - 1), total - largest - least * (count - 1)
    while rest > 0:
        movable = [i for i in range(1, count) if counts[i] < largest] or [i for i in range(1, count) if counts[i] < bound]
        mass, left = sum([loads[i] for i in movable]), rest
        for i in movable:
            extra = min(bound - counts[i], max(1, left * loads[i] // mass), rest)
            counts[i] = counts[i] + extra
            rest = rest - extra
    return np.array(counts)


def setup_inputs(seed: int = 0) -> dict:
    streams_of = jax.random.split(jax.random.key(seed), 7)
    teacher_new = draw_teacher_new(jax.random.fold_in(streams_of[6], 71), 0)
    queue = draw_queue(jax.random.fold_in(streams_of[6], 71), 0)
    student = draw_student(jax.random.fold_in(streams_of[6], 71), 0)
    prototypes = draw_prototypes(jax.random.fold_in(streams_of[6], 71), 0)
    owners_keys = jax.random.split(jax.random.fold_in(streams_of[4], 1), NEW_ROWS // NEW_DEV)
    owners_turns = jax.random.permutation(jax.random.fold_in(streams_of[4], 3), NEW_ROWS // NEW_DEV)
    owners = jax.vmap(lambda own, number: assign_block(jax.random.fold_in(streams_of[4], 2), own, number, NEW_DEV, N_SAMPLE, 1, CAP, 1))(owners_keys, owners_turns).reshape((NEW_ROWS, 1))
    queue_oldest_slot = jax.random.randint(streams_of[5], (N_SAMPLE,), 0, QUEUE_PER_INDEX).astype(jnp.int32)
    return dict(teacher_new=teacher_new, queue=queue, student=student, prototypes=prototypes, owners=owners, queue_oldest_slot=queue_oldest_slot)


teacher_temp = 0.07
student_temp = 0.1
epsilon = 1e-12

def unit_rows(values):
    widened = values.astype(jnp.float32)
    length = jnp.sqrt(lax.optimization_barrier(jnp.sum(widened * widened, axis=1, keepdims=True)) + epsilon)
    return (widened / length, length)

def against(left, right):
    return lax.dot_general(left, right, (((1,), (1,)), ((), ())), preferred_element_type=jnp.float32)

def reference(teacher_new, queue, student, prototypes, owners, queue_oldest_slot):
    teacher_hat = unit_rows(jnp.concatenate([teacher_new, queue], 0))[0].astype(jnp.bfloat16)
    proto_unit, proto_length = unit_rows(prototypes)
    proto_hat = proto_unit.astype(jnp.bfloat16)
    blocks = proto_hat.reshape(N_PROTO, K_DEV, FEATURE_WIDTH)
    exp_scores = lax.map(lambda block: jnp.exp(against(teacher_hat, block) / teacher_temp), blocks)
    row_scale = jnp.ones((TEACHERS,), jnp.float32)
    proto_scale = jnp.ones((N_PROTO, K_DEV), jnp.float32)
    for iteration in range(ITERS):
        column_sums = jnp.einsum('btk,t->bk', exp_scores, row_scale, precision=lax.Precision.HIGHEST)
        proto_scale = 1.0 / (PROTOTYPE_COUNT * column_sums)
        row_totals = jnp.einsum('btk,bk->t', exp_scores, proto_scale, precision=lax.Precision.HIGHEST)
        row_scale = 1.0 / (TEACHERS * row_totals)
    targets = exp_scores[:, :NEW_ROWS, :] * proto_scale[:, None, :] * row_scale[None, :NEW_ROWS, None] * TEACHERS
    student_normalized = unit_rows(student)[0].astype(jnp.bfloat16)
    logits = lax.map(lambda block: against(student_normalized, block) / student_temp, blocks)
    exp_logits = jnp.exp(logits)
    denominator = lax.optimization_barrier(jnp.sum(exp_logits, axis=(0, 2)))
    loss = (jnp.sum(jnp.log(denominator)) - jnp.sum(targets * logits)) / NEW_ROWS
    softmax_output = exp_logits / denominator[None, :, None]
    logit_gradient = (GRAD_SCALE * (softmax_output - targets) / (NEW_ROWS * student_temp)).astype(jnp.bfloat16)
    unit_gradient = jnp.einsum('plu,lr->pur', logit_gradient.astype(jnp.float32), student_normalized.astype(jnp.float32), precision=lax.Precision.HIGHEST).reshape(PROTOTYPE_COUNT, FEATURE_WIDTH)
    proto_grad = (unit_gradient - proto_unit * lax.optimization_barrier(jnp.sum(proto_unit * unit_gradient, axis=1, keepdims=True))) / proto_length
    owner_list = owners[:, 0].astype(jnp.int32)
    onehot = (owner_list[:, None] == jnp.arange(N_SAMPLE, dtype=jnp.int32)[None, :]).astype(jnp.int32)
    ranks = lax.optimization_barrier(jnp.sum((jnp.cumsum(onehot, axis=0).astype(jnp.int32) - onehot) * onehot, axis=1))
    heads = lax.optimization_barrier(jnp.sum(onehot * queue_oldest_slot.astype(jnp.int32)[None, :], axis=1))
    target_slot = owner_list * QUEUE_PER_INDEX + (heads + ranks) % QUEUE_PER_INDEX
    new_queue = queue.at[target_slot].set(teacher_new)
    return (new_queue, proto_grad, loss)
```

```python
import functools
import math

import jax
import jax.numpy as jnp
from jax import lax
from jax.experimental import pallas as pl
from jax.experimental.pallas import tpu as pltpu
from jax.sharding import PartitionSpec as P

ITERS = 3
LANES = 128
teacher_temp = 0.07
student_temp = 0.1
epsilon = 1e-12
LOG2E = math.log2(math.e)

f32, bf16 = jnp.float32, jnp.bfloat16
MESH = pl.DeviceIdType.MESH


def nt(left, right):
    return lax.dot_general(left, right, (((1,), (1,)), ((), ())), preferred_element_type=f32)


def nn(left, right):
    return lax.dot_general(left, right, (((1,), (0,)), ((), ())), preferred_element_type=f32)


def unit_rows(values):
    wide = values.astype(f32)
    squares = jnp.sum(wide * wide, axis=1, keepdims=True) + epsilon
    return wide * lax.rsqrt(squares)


def to_lanes(tile, first, rows):
    return jnp.concatenate([tile[r : r + 1, :] for r in range(first, first + rows)], axis=1)


def to_rows(vector):
    return [vector[:, c : c + LANES] for c in range(0, vector.shape[1], LANES)]


def padded(pieces, rows):
    have = sum(p.shape[0] for p in pieces)
    if have < rows:
        pieces = pieces + [jnp.zeros((rows - have, LANES), f32)]
    return jnp.concatenate(pieces, axis=0)


def high_low(vector):
    high = vector.astype(bf16).astype(f32)
    row = lax.broadcasted_iota(jnp.int32, (16, vector.shape[1]), 0)
    return jnp.where(row == 0, high, jnp.where(row == 1, vector - high, 0.0)).astype(bf16)


def joined(product):
    return product[0:1, :] + product[1:2, :]


def round8(n):
    return -(-n // 8) * 8


def wrap(index, n):
    return jnp.where(index >= n, index - n, index)


def kernel(
    n_proto, n_sample,
    tn_ref, q_ref, st_ref, pr_ref, ow_ref, head_ref,
    nq_ref, pg_ref, loss_ref,
    that, phat, sthat, es, bulk, stall, thall, y0buf, ybuf, rbuf, zbuf, pst, pscol, expl, uval,
    y0_send, y0_recv, y_send, y_recv, r_send, r_recv, z_send, z_recv,
    b_send, b_recv, w_send, w_recv,
):
    new, feat = tn_ref.shape
    ql = q_ref.shape[0]
    kdev = pr_ref.shape[0]
    tdev = new + ql
    half = new // 2
    nb, tb, kb = new // LANES, tdev // LANES, kdev // LANES
    share = kdev // n_sample
    n_new = new * n_sample
    protos_total = kdev * n_proto
    teachers_total = float(tdev * n_sample)
    blk = min(256, share)
    me_p, me_s = lax.axis_index("proto"), lax.axis_index("sample")
    core = lax.rem(me_p, 2)
    sibling = me_p + 1 - 2 * core

    def p_peers():
        return [wrap(me_p + d, n_proto) for d in range(1, n_proto)]

    def s_peers():
        return [wrap(me_s + d, n_sample) for d in range(1, n_sample)]

    barrier = pltpu.get_barrier_semaphore()
    for p in p_peers():
        pl.semaphore_signal(barrier, inc=1, device_id={"proto": p}, device_id_type=MESH)
    for s in s_peers():
        pl.semaphore_signal(barrier, inc=1, device_id={"sample": s}, device_id_type=MESH)

    def send_s(src, dst, ssem, rsem):
        for s in s_peers():
            pltpu.make_async_remote_copy(src, dst, ssem, rsem, device_id={"sample": s}, device_id_type=MESH).start()

    def send_p(src, dst, ssem, rsem):
        for p in p_peers():
            pltpu.make_async_remote_copy(src, dst, ssem, rsem, device_id={"proto": p}, device_id_type=MESH).start()

    def whole(ref, count, ssem, rsem):
        view = ref.at[pl.ds(0, count)]
        return pltpu.make_async_remote_copy(view, view, ssem, rsem, device_id={"proto": sibling}, device_id_type=MESH)

    student = unit_rows(st_ref[...]).astype(bf16)
    sthat[...] = student
    for h in range(2):
        bulk[me_s, h, 0] = student[h * half : (h + 1) * half]
        bulk[me_s, h, 1] = tn_ref[h * half : (h + 1) * half, :]

    that[0:new, :] = unit_rows(tn_ref[...]).astype(bf16)
    that[new:tdev, :] = unit_rows(q_ref[...]).astype(bf16)

    pl.semaphore_wait(barrier, n_proto - 1 + n_sample - 1)
    for d in range(1, n_sample):
        pltpu.make_async_remote_copy(
            bulk.at[me_s, core], bulk.at[me_s, core], b_send.at[d], b_recv.at[d],
            device_id={"sample": wrap(me_s + d, n_sample)}, device_id_type=MESH,
        ).start()

    pb = 256

    def score_block(b, carry):
        at = pl.multiple_of(b * pb, pb)
        unit = unit_rows(pr_ref[pl.ds(at, pb), :]).astype(bf16)
        phat[pl.ds(at, pb), :] = unit
        e = jnp.exp2(nt(that[...], unit) * (LOG2E / teacher_temp))
        es[new:, pl.ds(at, pb)] = e.astype(bf16)
        sums = jnp.sum(e, axis=0, keepdims=True)
        for c, row in enumerate(to_rows(sums)):
            y0buf[me_s, pl.ds(b * (pb // LANES) + c, 1), :] = row
        return carry

    lax.fori_loop(0, kdev // pb, score_block, 0)
    y0buf[me_s, kb:, :] = padded([ow_ref[...].astype(f32)], round8(nb))
    send_s(y0buf.at[me_s], y0buf.at[me_s], y0_send, y0_recv)

    def student_block(b, denominator):
        at = pl.multiple_of(b * pb, pb)
        unit = phat[pl.ds(at, pb), :]
        logits = nt(sthat[...], unit) * (1.0 / student_temp)
        es[0:new, pl.ds(at, pb)] = (es[new : 2 * new, pl.ds(at, pb)].astype(f32) * logits).astype(bf16)
        across = nt(unit, sthat[...]) * (LOG2E / student_temp)
        return denominator + jnp.sum(jnp.exp2(across), axis=0, keepdims=True)

    denominator = lax.fori_loop(0, kdev // pb, student_block, jnp.zeros((1, new), f32))

    whole(y0buf, n_sample - 1, y0_send, y0_recv).wait_recv()
    columns = jnp.sum(y0buf[:, 0:kb, :], axis=0)
    scale_tile = 1.0 / (float(protos_total) * columns)

    def row_totals(tile, first, rows):
        left = high_low(to_lanes(tile, 0, kb))
        return jnp.concatenate([joined(nt(left, es[r : r + 256, :])) for r in range(first, first + rows, 256)], axis=1)

    def column_sums(tile):
        left = high_low(to_lanes(tile, 0, tb))
        return jnp.concatenate([joined(nn(left, es[new:, c : c + 256])) for c in range(0, kdev, 256)], axis=1)

    def gather_new():
        for s in range(n_sample):
            for h in range(2):
                at = s * new + h * half
                stall[at : at + half, :] = bulk[s, h, 0]
                thall[at : at + half, :] = unit_rows(bulk[s, h, 1]).astype(bf16)

    def refill():
        head = head_ref[0].astype(f32)
        before = lax.broadcasted_iota(jnp.int32, (LANES, LANES), 0) < lax.broadcasted_iota(jnp.int32, (LANES, LANES), 1)
        before = before.astype(f32).astype(bf16)
        slots = lax.broadcasted_iota(jnp.int32, (ql, LANES), 0)
        mine = me_s.astype(f32)
        offset = jnp.zeros((1, 1), f32)
        rows = jnp.zeros((ql, feat), f32)
        hit = jnp.zeros((ql, 1), f32)
        per_half = nb // 2
        for s in range(n_sample):
            for c in range(nb):
                own = (y0buf[s, kb + c : kb + c + 1, :] == mine).astype(f32)
                rank = nn(jnp.broadcast_to(own, (16, LANES)).astype(bf16), before)[0:1, :] + offset
                offset = offset + jnp.sum(own, axis=1, keepdims=True)
                slot = head + rank
                slot = jnp.where(slot >= float(ql), slot - float(ql), slot)
                slot = jnp.where(own > 0.0, slot, -1.0).astype(jnp.int32)
                chosen = (slots == slot).astype(f32)
                hit = hit + jnp.sum(chosen, axis=1, keepdims=True)
                h, inner = c // per_half, (c % per_half) * LANES
                rows = rows + nn(chosen.astype(bf16), bulk[s, h, 1, inner : inner + LANES, :])
        nq_ref[...] = jnp.where(hit > 0.0, rows, q_ref[...].astype(f32)).astype(bf16)

    first_row = pl.multiple_of(me_s * share, share)

    def own_block(b, carry):
        at = pl.multiple_of(b * blk, blk)
        unit = phat[pl.ds(first_row + at, blk), :]
        for s in range(n_sample):
            span = slice(s * new, (s + 1) * new)
            expl[pl.ds(at, blk), span] = jnp.exp2(nt(unit, stall[span, :]) * (LOG2E / student_temp))
            uval[pl.ds(at, blk), span] = jnp.exp2(nt(unit, thall[span, :]) * (LOG2E / teacher_temp))
        return carry

    for step in range(ITERS - 1):
        totals = row_totals(scale_tile, new, tdev)
        rbuf[step, me_p] = padded(to_rows(totals), tb)
        send_p(rbuf.at[step, me_p], rbuf.at[step, me_p], r_send.at[step], r_recv.at[step])
        if step == 0:
            for d in range(1, n_sample):
                s = wrap(me_s + n_sample - d, n_sample)
                arrived = bulk.at[s, core]
                pltpu.make_async_remote_copy(arrived, arrived, b_send.at[d], b_recv.at[d], device_id={"proto": sibling}, device_id_type=MESH).wait_recv()
                pltpu.make_async_remote_copy(arrived, arrived, w_send.at[d], w_recv.at[d], device_id={"proto": sibling}, device_id_type=MESH).start()
        else:
            for d in range(1, n_sample):
                s = wrap(me_s + n_sample - d, n_sample)
                other = bulk.at[s, 1 - core]
                pltpu.make_async_remote_copy(other, other, w_send.at[d], w_recv.at[d], device_id={"proto": sibling}, device_id_type=MESH).wait_recv()
            gather_new()
            refill()
        whole(rbuf.at[step], n_proto - 1, r_send.at[step], r_recv.at[step]).wait_recv()
        row_tile = 1.0 / (teachers_total * jnp.sum(rbuf[step], axis=0))
        ybuf[step, me_s] = padded(to_rows(column_sums(row_tile)), kb)
        send_s(ybuf.at[step, me_s], ybuf.at[step, me_s], y_send.at[step], y_recv.at[step])
        if step == ITERS - 2:
            lax.fori_loop(0, share // blk, own_block, 0)
        whole(ybuf.at[step], n_sample - 1, y_send.at[step], y_recv.at[step]).wait_recv()
        scale_tile = 1.0 / (float(protos_total) * jnp.sum(ybuf[step], axis=0))

    totals = row_totals(scale_tile, 0, 2 * new)
    last = padded(to_rows(totals) + to_rows(denominator), rbuf.shape[2])
    final = ITERS - 1
    rbuf[final, me_p] = last
    send_p(rbuf.at[final, me_p], rbuf.at[final, me_p], r_send.at[final], r_recv.at[final])

    pst[...] = scale_tile
    for r in range(share // LANES):
        row = pst[pl.ds(me_s * (share // LANES) + r, 1), :]
        pscol[r * LANES : (r + 1) * LANES, :] = jnp.transpose(jnp.broadcast_to(row, (LANES, LANES)))

    def scale_block(b, carry):
        at = pl.multiple_of(b * blk, blk)
        column = pscol[pl.ds(at, blk), :]
        for c in range(0, n_new, LANES):
            uval[pl.ds(at, blk), c : c + LANES] = uval[pl.ds(at, blk), c : c + LANES] * column
        return carry

    lax.fori_loop(0, share // blk, scale_block, 0)

    whole(rbuf.at[final], n_proto - 1, r_send.at[final], r_recv.at[final]).wait_recv()
    summed = jnp.sum(rbuf[final], axis=0)
    scaled = 1.0 / summed[nb : 2 * nb, :]
    denominators = summed[2 * nb : 3 * nb, :]
    cross = jnp.log(denominators) - scaled * summed[0:nb, :]
    cross = jnp.sum(jnp.sum(cross, axis=0, keepdims=True), axis=1, keepdims=True)
    grad_scale = float(protos_total * new // 32) / (n_new * student_temp)
    zbuf[me_s] = padded(
        [grad_scale * scaled, grad_scale / denominators, jnp.broadcast_to(cross, (1, LANES))],
        zbuf.shape[1],
    )
    send_s(zbuf.at[me_s], zbuf.at[me_s], z_send, z_recv)
    whole(zbuf, n_sample - 1, z_send, z_recv).wait_recv()
    terms = zbuf[...]
    loss = terms[0, 2 * nb : 2 * nb + 1, 0:1]
    for s in range(1, n_sample):
        loss = loss + terms[s, 2 * nb : 2 * nb + 1, 0:1]
    loss_ref[...] = loss / float(n_new)
    row_scale = jnp.concatenate([to_lanes(terms[s], 0, nb) for s in range(n_sample)], axis=1)
    soft_scale = jnp.concatenate([to_lanes(terms[s], nb, nb) for s in range(n_sample)], axis=1)

    def gradient_block(b, carry):
        at = pl.multiple_of(b * blk, blk)
        rows = pl.ds(at, blk)
        gradient = (expl[rows, :] * soft_scale - uval[rows, :] * row_scale).astype(bf16)
        unit_gradient = nn(gradient, stall[...])
        wide = pr_ref[pl.ds(first_row + at, blk), :].astype(f32)
        inverse = lax.rsqrt(jnp.sum(wide * wide, axis=1, keepdims=True) + epsilon)
        unit = wide * inverse
        along = jnp.sum(unit * unit_gradient, axis=1, keepdims=True)
        pg_ref[rows, :] = (unit_gradient - unit * along) * inverse
        return carry

    lax.fori_loop(0, share // blk, gradient_block, 0)

    whole(y0buf, n_sample - 1, y0_send, y0_recv).wait_send()
    for step in range(ITERS - 1):
        whole(ybuf.at[step], n_sample - 1, y_send.at[step], y_recv.at[step]).wait_send()
    for step in range(ITERS):
        whole(rbuf.at[step], n_proto - 1, r_send.at[step], r_recv.at[step]).wait_send()
    whole(zbuf, n_sample - 1, z_send, z_recv).wait_send()
    for d in range(1, n_sample):
        mine = bulk.at[me_s, core]
        pltpu.make_async_remote_copy(mine, mine, b_send.at[d], b_recv.at[d], device_id={"proto": sibling}, device_id_type=MESH).wait_send()
        pltpu.make_async_remote_copy(mine, mine, w_send.at[d], w_recv.at[d], device_id={"proto": sibling}, device_id_type=MESH).wait_send()


def on_device(n_proto, n_sample, teacher_new, queue, student, prototypes, owners, queue_oldest_slot):
    new, feat = teacher_new.shape
    ql, kdev = queue.shape[0], prototypes.shape[0]
    tdev = new + ql
    nb, tb, kb = new // LANES, tdev // LANES, kdev // LANES
    share = kdev // n_sample
    n_new = new * n_sample
    vmem = pl.BlockSpec(memory_space=pltpu.VMEM)
    smem = pl.BlockSpec(memory_space=pltpu.SMEM)
    dma = pltpu.SemaphoreType.DMA
    rows = max(round8(tb), round8(3 * nb))
    new_queue, proto_grad, loss = pl.pallas_call(
        functools.partial(kernel, n_proto, n_sample),
        out_shape=(
            jax.ShapeDtypeStruct((ql, feat), bf16),
            jax.ShapeDtypeStruct((share, feat), f32),
            jax.ShapeDtypeStruct((1, 1), f32),
        ),
        in_specs=[vmem] * 5 + [smem],
        out_specs=(vmem, vmem, vmem),
        scratch_shapes=[
            pltpu.VMEM((tdev, feat), bf16),
            pltpu.VMEM((kdev, feat), bf16),
            pltpu.VMEM((new, feat), bf16),
            pltpu.VMEM((new + tdev, kdev), bf16),
            pltpu.VMEM((n_sample, 2, 2, new // 2, feat), bf16),
            pltpu.VMEM((n_new, feat), bf16),
            pltpu.VMEM((n_new, feat), bf16),
            pltpu.VMEM((n_sample, kb + round8(nb), LANES), f32),
            pltpu.VMEM((ITERS - 1, n_sample, kb, LANES), f32),
            pltpu.VMEM((ITERS, n_proto, rows, LANES), f32),
            pltpu.VMEM((n_sample, round8(2 * nb + 1), LANES), f32),
            pltpu.VMEM((kb, LANES), f32),
            pltpu.VMEM((share, LANES), f32),
            pltpu.VMEM((share, n_new), f32),
            pltpu.VMEM((share, n_new), f32),
            dma, dma,
            dma((ITERS - 1,)), dma((ITERS - 1,)),
            dma((ITERS,)), dma((ITERS,)),
            dma, dma,
            dma((n_sample,)), dma((n_sample,)),
            dma((n_sample,)), dma((n_sample,)),
        ],
        compiler_params=pltpu.CompilerParams(
            collective_id=0, has_side_effects=True, vmem_limit_bytes=48 * 1024 * 1024
        ),
    )(teacher_new, queue, student, prototypes, owners.reshape(nb, LANES), queue_oldest_slot)
    return new_queue, proto_grad, loss.reshape(())


def solution(mesh):
    in_specs = (
        P("sample", None),
        P("sample", None),
        P("sample", None),
        P("proto", None),
        P("sample", None),
        P("sample"),
    )
    out_specs = (P("sample", None), P(("proto", "sample"), None), P())
    body = functools.partial(on_device, mesh.shape["proto"], mesh.shape["sample"])
    return jax.shard_map(body, mesh=mesh, in_specs=in_specs, out_specs=out_specs, check_vma=False)
```

```python
import functools
import math

import jax
import jax.numpy as jnp
from jax import lax
from jax.experimental import pallas as pl
from jax.experimental.pallas import tpu as pltpu
from jax.sharding import PartitionSpec as P

ITERS = 3
LANES = 128
teacher_temp = 0.07
student_temp = 0.1
epsilon = 1e-12
LOG2E = math.log2(math.e)

f32, bf16 = jnp.float32, jnp.bfloat16
MESH = pl.DeviceIdType.MESH


def nt(left, right):
    return lax.dot_general(left, right, (((1,), (1,)), ((), ())), preferred_element_type=f32)


def nn(left, right):
    return lax.dot_general(left, right, (((1,), (0,)), ((), ())), preferred_element_type=f32)


def unit_rows(values):
    wide = values.astype(f32)
    squares = jnp.sum(wide * wide, axis=1, keepdims=True) + epsilon
    return wide * lax.rsqrt(squares)


def to_lanes(tile, first, rows):
    return jnp.concatenate([tile[r : r + 1, :] for r in range(first, first + rows)], axis=1)


def to_rows(vector):
    return [vector[:, c : c + LANES] for c in range(0, vector.shape[1], LANES)]


def padded(pieces, rows):
    have = sum(p.shape[0] for p in pieces)
    if have < rows:
        pieces = pieces + [jnp.zeros((rows - have, LANES), f32)]
    return jnp.concatenate(pieces, axis=0)


def high_low(vector):
    high = vector.astype(bf16).astype(f32)
    row = lax.broadcasted_iota(jnp.int32, (16, vector.shape[1]), 0)
    return jnp.where(row == 0, high, jnp.where(row == 1, vector - high, 0.0)).astype(bf16)


def joined(product):
    return product[0:1, :] + product[1:2, :]


def round8(n):
    return -(-n // 8) * 8


def wrap(index, n):
    return jnp.where(index >= n, index - n, index)


def kernel(
    n_proto, n_sample,
    tn_hbm, q_hbm, st_hbm, pr_hbm, ow_hbm, head_ref,
    nq_ref, pg_ref, loss_ref,
    tn_ref, q_ref, st_ref, pr_ref, ow_ref, in_sem,
    that, phat, sthat, es, bulk, stall, thall, y0buf, ybuf, rbuf, zbuf, pst, pscol, expl, uval,
    y0_send, y0_recv, y_send, y_recv, r_send, r_recv, z_send, z_recv,
    b_send, b_recv, w_send, w_recv,
):
    new, feat = tn_ref.shape
    ql = q_ref.shape[0]
    kdev = pr_ref.shape[0]
    tdev = new + ql
    half = new // 2
    nb, tb, kb = new // LANES, tdev // LANES, kdev // LANES
    share = kdev // n_sample
    n_new = new * n_sample
    protos_total = kdev * n_proto
    teachers_total = float(tdev * n_sample)
    blk = min(256, share)
    me_p, me_s = lax.axis_index("proto"), lax.axis_index("sample")
    core = lax.rem(me_p, 2)
    sibling = me_p + 1 - 2 * core

    def p_peers():
        return [wrap(me_p + d, n_proto) for d in range(1, n_proto)]

    def s_peers():
        return [wrap(me_s + d, n_sample) for d in range(1, n_sample)]

    arriving = [
        pltpu.make_async_copy(there, here, in_sem.at[i])
        for i, (there, here) in enumerate(
            [(st_hbm, st_ref), (tn_hbm, tn_ref), (q_hbm, q_ref), (pr_hbm, pr_ref), (ow_hbm, ow_ref)]
        )
    ]
    for copy in arriving:
        copy.start()

    barrier = pltpu.get_barrier_semaphore()
    for p in p_peers():
        pl.semaphore_signal(barrier, inc=1, device_id={"proto": p}, device_id_type=MESH)
    for s in s_peers():
        pl.semaphore_signal(barrier, inc=1, device_id={"sample": s}, device_id_type=MESH)

    def send_s(src, dst, ssem, rsem):
        for s in s_peers():
            pltpu.make_async_remote_copy(src, dst, ssem, rsem, device_id={"sample": s}, device_id_type=MESH).start()

    def send_p(src, dst, ssem, rsem):
        for p in p_peers():
            pltpu.make_async_remote_copy(src, dst, ssem, rsem, device_id={"proto": p}, device_id_type=MESH).start()

    def whole(ref, count, ssem, rsem):
        view = ref.at[pl.ds(0, count)]
        return pltpu.make_async_remote_copy(view, view, ssem, rsem, device_id={"proto": sibling}, device_id_type=MESH)

    arriving[0].wait()
    arriving[1].wait()
    student = unit_rows(st_ref[...]).astype(bf16)
    sthat[...] = student
    for h in range(2):
        bulk[me_s, h, 0] = student[h * half : (h + 1) * half]
        bulk[me_s, h, 1] = tn_ref[h * half : (h + 1) * half, :]

    that[0:new, :] = unit_rows(tn_ref[...]).astype(bf16)
    arriving[2].wait()
    that[new:tdev, :] = unit_rows(q_ref[...]).astype(bf16)

    arriving[3].wait()
    arriving[4].wait()
    pl.semaphore_wait(barrier, n_proto - 1 + n_sample - 1)
    for d in range(1, n_sample):
        pltpu.make_async_remote_copy(
            bulk.at[me_s, core], bulk.at[me_s, core], b_send.at[d], b_recv.at[d],
            device_id={"sample": wrap(me_s + d, n_sample)}, device_id_type=MESH,
        ).start()

    pb = 256

    def score_block(b, carry):
        at = pl.multiple_of(b * pb, pb)
        unit = unit_rows(pr_ref[pl.ds(at, pb), :]).astype(bf16)
        phat[pl.ds(at, pb), :] = unit
        e = jnp.exp2(nt(that[...], unit) * (LOG2E / teacher_temp))
        es[new:, pl.ds(at, pb)] = e.astype(bf16)
        sums = jnp.sum(e, axis=0, keepdims=True)
        for c, row in enumerate(to_rows(sums)):
            y0buf[me_s, pl.ds(b * (pb // LANES) + c, 1), :] = row
        return carry

    lax.fori_loop(0, kdev // pb, score_block, 0, unroll=2)
    y0buf[me_s, kb:, :] = padded([ow_ref[...].astype(f32)], round8(nb))
    send_s(y0buf.at[me_s], y0buf.at[me_s], y0_send, y0_recv)

    def student_block(b, denominator):
        at = pl.multiple_of(b * pb, pb)
        unit = phat[pl.ds(at, pb), :]
        logits = nt(sthat[...], unit) * (1.0 / student_temp)
        es[0:new, pl.ds(at, pb)] = (es[new : 2 * new, pl.ds(at, pb)].astype(f32) * logits).astype(bf16)
        across = nt(unit, sthat[...]) * (LOG2E / student_temp)
        return denominator + jnp.sum(jnp.exp2(across), axis=0, keepdims=True)

    denominator = lax.fori_loop(0, kdev // pb, student_block, jnp.zeros((1, new), f32))

    whole(y0buf, n_sample - 1, y0_send, y0_recv).wait_recv()
    columns = jnp.sum(y0buf[:, 0:kb, :], axis=0)
    scale_tile = 1.0 / (float(protos_total) * columns)

    def row_totals(tile, first, rows):
        left = high_low(to_lanes(tile, 0, kb))
        return jnp.concatenate([joined(nt(left, es[r : r + 256, :])) for r in range(first, first + rows, 256)], axis=1)

    def column_sums(tile):
        left = high_low(to_lanes(tile, 0, tb))
        return jnp.concatenate([joined(nn(left, es[new:, c : c + 256])) for c in range(0, kdev, 256)], axis=1)

    def gather_new():
        for s in range(n_sample):
            for h in range(2):
                at = s * new + h * half
                stall[at : at + half, :] = bulk[s, h, 0]
                thall[at : at + half, :] = unit_rows(bulk[s, h, 1]).astype(bf16)

    def refill():
        head = head_ref[0].astype(f32)
        before = lax.broadcasted_iota(jnp.int32, (LANES, LANES), 0) < lax.broadcasted_iota(jnp.int32, (LANES, LANES), 1)
        before = before.astype(f32).astype(bf16)
        slots = lax.broadcasted_iota(jnp.int32, (ql, LANES), 0)
        mine = me_s.astype(f32)
        offset = jnp.zeros((1, 1), f32)
        rows = jnp.zeros((ql, feat), f32)
        hit = jnp.zeros((ql, 1), f32)
        per_half = nb // 2
        for s in range(n_sample):
            for c in range(nb):
                own = (y0buf[s, kb + c : kb + c + 1, :] == mine).astype(f32)
                rank = nn(jnp.broadcast_to(own, (16, LANES)).astype(bf16), before)[0:1, :] + offset
                offset = offset + jnp.sum(own, axis=1, keepdims=True)
                slot = head + rank
                slot = jnp.where(slot >= float(ql), slot - float(ql), slot)
                slot = jnp.where(own > 0.0, slot, -1.0).astype(jnp.int32)
                chosen = (slots == slot).astype(f32)
                hit = hit + jnp.sum(chosen, axis=1, keepdims=True)
                h, inner = c // per_half, (c % per_half) * LANES
                rows = rows + nn(chosen.astype(bf16), bulk[s, h, 1, inner : inner + LANES, :])
        nq_ref[...] = jnp.where(hit > 0.0, rows, q_ref[...].astype(f32)).astype(bf16)

    first_row = pl.multiple_of(me_s * share, share)

    def own_block(b, carry):
        at = pl.multiple_of(b * blk, blk)
        unit = phat[pl.ds(first_row + at, blk), :]
        for s in range(n_sample):
            span = slice(s * new, (s + 1) * new)
            expl[pl.ds(at, blk), span] = jnp.exp2(nt(unit, stall[span, :]) * (LOG2E / student_temp))
            uval[pl.ds(at, blk), span] = jnp.exp2(nt(unit, thall[span, :]) * (LOG2E / teacher_temp))
        return carry

    for step in range(ITERS - 1):
        totals = row_totals(scale_tile, new, tdev)
        rbuf[step, me_p] = padded(to_rows(totals), tb)
        send_p(rbuf.at[step, me_p], rbuf.at[step, me_p], r_send.at[step], r_recv.at[step])
        if step == 0:
            for d in range(1, n_sample):
                s = wrap(me_s + n_sample - d, n_sample)
                arrived = bulk.at[s, core]
                pltpu.make_async_remote_copy(arrived, arrived, b_send.at[d], b_recv.at[d], device_id={"proto": sibling}, device_id_type=MESH).wait_recv()
                pltpu.make_async_remote_copy(arrived, arrived, w_send.at[d], w_recv.at[d], device_id={"proto": sibling}, device_id_type=MESH).start()
        else:
            for d in range(1, n_sample):
                s = wrap(me_s + n_sample - d, n_sample)
                other = bulk.at[s, 1 - core]
                pltpu.make_async_remote_copy(other, other, w_send.at[d], w_recv.at[d], device_id={"proto": sibling}, device_id_type=MESH).wait_recv()
            gather_new()
            refill()
        whole(rbuf.at[step], n_proto - 1, r_send.at[step], r_recv.at[step]).wait_recv()
        row_tile = 1.0 / (teachers_total * jnp.sum(rbuf[step], axis=0))
        ybuf[step, me_s] = padded(to_rows(column_sums(row_tile)), kb)
        send_s(ybuf.at[step, me_s], ybuf.at[step, me_s], y_send.at[step], y_recv.at[step])
        if step == ITERS - 2:
            lax.fori_loop(0, share // blk, own_block, 0)
        whole(ybuf.at[step], n_sample - 1, y_send.at[step], y_recv.at[step]).wait_recv()
        scale_tile = 1.0 / (float(protos_total) * jnp.sum(ybuf[step], axis=0))

    totals = row_totals(scale_tile, 0, 2 * new)
    last = padded(to_rows(totals) + to_rows(denominator), rbuf.shape[2])
    final = ITERS - 1
    rbuf[final, me_p] = last
    send_p(rbuf.at[final, me_p], rbuf.at[final, me_p], r_send.at[final], r_recv.at[final])

    pst[...] = scale_tile
    for r in range(share // LANES):
        row = pst[pl.ds(me_s * (share // LANES) + r, 1), :]
        pscol[r * LANES : (r + 1) * LANES, :] = jnp.transpose(jnp.broadcast_to(row, (LANES, LANES)))

    def scale_block(b, carry):
        at = pl.multiple_of(b * blk, blk)
        column = pscol[pl.ds(at, blk), :]
        for c in range(0, n_new, LANES):
            uval[pl.ds(at, blk), c : c + LANES] = uval[pl.ds(at, blk), c : c + LANES] * column
        return carry

    lax.fori_loop(0, share // blk, scale_block, 0)

    whole(rbuf.at[final], n_proto - 1, r_send.at[final], r_recv.at[final]).wait_recv()
    summed = jnp.sum(rbuf[final], axis=0)
    scaled = 1.0 / summed[nb : 2 * nb, :]
    denominators = summed[2 * nb : 3 * nb, :]
    cross = jnp.log(denominators) - scaled * summed[0:nb, :]
    cross = jnp.sum(jnp.sum(cross, axis=0, keepdims=True), axis=1, keepdims=True)
    grad_scale = float(protos_total * new // 32) / (n_new * student_temp)
    zbuf[me_s] = padded(
        [grad_scale * scaled, grad_scale / denominators, jnp.broadcast_to(cross, (1, LANES))],
        zbuf.shape[1],
    )
    send_s(zbuf.at[me_s], zbuf.at[me_s], z_send, z_recv)
    whole(zbuf, n_sample - 1, z_send, z_recv).wait_recv()
    terms = zbuf[...]
    loss = terms[0, 2 * nb : 2 * nb + 1, 0:1]
    for s in range(1, n_sample):
        loss = loss + terms[s, 2 * nb : 2 * nb + 1, 0:1]
    loss_ref[...] = loss / float(n_new)
    row_scale = jnp.concatenate([to_lanes(terms[s], 0, nb) for s in range(n_sample)], axis=1)
    soft_scale = jnp.concatenate([to_lanes(terms[s], nb, nb) for s in range(n_sample)], axis=1)

    def gradient_block(b, carry):
        at = pl.multiple_of(b * blk, blk)
        rows = pl.ds(at, blk)
        gradient = (expl[rows, :] * soft_scale - uval[rows, :] * row_scale).astype(bf16)
        unit_gradient = nn(gradient, stall[...])
        wide = pr_ref[pl.ds(first_row + at, blk), :].astype(f32)
        inverse = lax.rsqrt(jnp.sum(wide * wide, axis=1, keepdims=True) + epsilon)
        unit = wide * inverse
        along = jnp.sum(unit * unit_gradient, axis=1, keepdims=True)
        pg_ref[rows, :] = (unit_gradient - unit * along) * inverse
        return carry

    lax.fori_loop(0, share // blk, gradient_block, 0, unroll=2 if share // blk > 1 else 1)

    whole(y0buf, n_sample - 1, y0_send, y0_recv).wait_send()
    for step in range(ITERS - 1):
        whole(ybuf.at[step], n_sample - 1, y_send.at[step], y_recv.at[step]).wait_send()
    for step in range(ITERS):
        whole(rbuf.at[step], n_proto - 1, r_send.at[step], r_recv.at[step]).wait_send()
    whole(zbuf, n_sample - 1, z_send, z_recv).wait_send()
    for d in range(1, n_sample):
        mine = bulk.at[me_s, core]
        pltpu.make_async_remote_copy(mine, mine, b_send.at[d], b_recv.at[d], device_id={"proto": sibling}, device_id_type=MESH).wait_send()
        pltpu.make_async_remote_copy(mine, mine, w_send.at[d], w_recv.at[d], device_id={"proto": sibling}, device_id_type=MESH).wait_send()


def on_device(n_proto, n_sample, teacher_new, queue, student, prototypes, owners, queue_oldest_slot):
    new, feat = teacher_new.shape
    ql, kdev = queue.shape[0], prototypes.shape[0]
    tdev = new + ql
    nb, tb, kb = new // LANES, tdev // LANES, kdev // LANES
    share = kdev // n_sample
    n_new = new * n_sample
    vmem = pl.BlockSpec(memory_space=pltpu.VMEM)
    smem = pl.BlockSpec(memory_space=pltpu.SMEM)
    dma = pltpu.SemaphoreType.DMA
    rows = max(round8(tb), round8(3 * nb))
    new_queue, proto_grad, loss = pl.pallas_call(
        functools.partial(kernel, n_proto, n_sample),
        out_shape=(
            jax.ShapeDtypeStruct((ql, feat), bf16),
            jax.ShapeDtypeStruct((share, feat), f32),
            jax.ShapeDtypeStruct((1, 1), f32),
        ),
        in_specs=[pl.BlockSpec(memory_space=pltpu.HBM)] * 5 + [smem],
        out_specs=(vmem, vmem, vmem),
        scratch_shapes=[
            pltpu.VMEM((new, feat), bf16),
            pltpu.VMEM((ql, feat), bf16),
            pltpu.VMEM((new, feat), bf16),
            pltpu.VMEM((kdev, feat), bf16),
            pltpu.VMEM((nb, LANES), jnp.int32),
            dma((5,)),
            pltpu.VMEM((tdev, feat), bf16),
            pltpu.VMEM((kdev, feat), bf16),
            pltpu.VMEM((new, feat), bf16),
            pltpu.VMEM((new + tdev, kdev), bf16),
            pltpu.VMEM((n_sample, 2, 2, new // 2, feat), bf16),
            pltpu.VMEM((n_new, feat), bf16),
            pltpu.VMEM((n_new, feat), bf16),
            pltpu.VMEM((n_sample, kb + round8(nb), LANES), f32),
            pltpu.VMEM((ITERS - 1, n_sample, kb, LANES), f32),
            pltpu.VMEM((ITERS, n_proto, rows, LANES), f32),
            pltpu.VMEM((n_sample, round8(2 * nb + 1), LANES), f32),
            pltpu.VMEM((kb, LANES), f32),
            pltpu.VMEM((share, LANES), f32),
            pltpu.VMEM((share, n_new), f32),
            pltpu.VMEM((share, n_new), f32),
            dma, dma,
            dma((ITERS - 1,)), dma((ITERS - 1,)),
            dma((ITERS,)), dma((ITERS,)),
            dma, dma,
            dma((n_sample,)), dma((n_sample,)),
            dma((n_sample,)), dma((n_sample,)),
        ],
        compiler_params=pltpu.CompilerParams(
            collective_id=0, has_side_effects=True, vmem_limit_bytes=62 * 1024 * 1024
        ),
    )(teacher_new, queue, student, prototypes, owners.reshape(nb, LANES), queue_oldest_slot)
    return new_queue, proto_grad, loss.reshape(())


def solution(mesh):
    in_specs = (
        P("sample", None),
        P("sample", None),
        P("sample", None),
        P("proto", None),
        P("sample", None),
        P("sample"),
    )
    out_specs = (P("sample", None), P(("proto", "sample"), None), P())
    body = functools.partial(on_device, mesh.shape["proto"], mesh.shape["sample"])
    return jax.shard_map(body, mesh=mesh, in_specs=in_specs, out_specs=out_specs, check_vma=False)
```
